256 devices in a mesh: row: 32 (over z_hi, y, x), col: 8 (over z_lo, core).
Axes of the slice: x: 4, y: 4, z: 8 (z_hi: 2, z_lo: 4; z = z_hi * 4 + z_lo), core: 2. Of those that a mesh axis runs over, the one named last changes fastest.
Arguments:
- tokens: bfloat16 [5120, 3072], P('row', 'col'), may hold values from -6 to 6
- up_weight: bfloat16 [3072, 12288], P('row', 'col'), may hold values from -0.109375 to 0.109375
- down_weight: bfloat16 [12288, 3072], P('col', 'row'), may hold values from -0.0546875 to 0.0546875
Outputs:
- projected: bfloat16 [5120, 3072], P('row', 'col')
The draws below stay inside these ranges and needn't reach their ends.
All inputs are finite; a program needn't handle non-finite values.
Results may differ from the reference program's by a relative error of at most 0.0049.
Values may be sent and summed in bfloat16 or wider, within the bound.
A program may use at most 128 MiB of HBM per device.

```python
import jax
import jax.numpy as jnp

D = 3072
FF = 12288
TOKENS = 5120


def shard_levels(key, shape, pieces, least, largest):
    level = 1.0
    for position, blocks in pieces:
        heights = jax.random.uniform(jax.random.fold_in(jax.random.fold_in(key, 6), position), (blocks,), jnp.float32, least / len(pieces), largest / len(pieces))
        level = level * jnp.repeat(jnp.exp(heights), shape[position] // blocks).reshape((-1,) + (1,) * (len(shape) - 1 - position))
    return level


def normal_values(key, shape, scale, reach, cuts=(), kind=jnp.bfloat16):
    array = jax.random.normal(key, shape, jnp.float32) * scale
    if len(cuts) > 0:
        array = shard_levels(key, shape, cuts, -0.22, 0.18) * array
    return jnp.clip(array, min=-reach, max=reach).astype(kind)


def setup_inputs(seed: int = 0) -> dict:
    arg_keys = jax.random.split(jax.random.key(seed), 4)
    tokens = normal_values(arg_keys[0], (TOKENS, D), 1.0, 6.0, ((0, 32), (1, 8)))
    up_weight = normal_values(arg_keys[1], (D, FF), D ** -0.5, 0.109375, ((0, 32), (1, 8)))
    down_weight = normal_values(arg_keys[2], (FF, D), FF ** -0.5, 0.0546875, ((0, 8), (1, 32)))
    return dict(tokens=tokens, up_weight=up_weight, down_weight=down_weight)


def reference(tokens, up_weight, down_weight):
    pre = jnp.dot(tokens, up_weight, preferred_element_type=jnp.float32)
    hidden = jax.nn.gelu(pre, approximate=False).astype(jnp.bfloat16)
    return jnp.dot(hidden, down_weight, preferred_element_type=jnp.float32).astype(jnp.bfloat16)
```

```python
import jax
import jax.numpy as jnp
from jax import lax
from jax.experimental import pallas as pl
from jax.experimental.pallas import tpu as pltpu
from jax.sharding import PartitionSpec as P

MESH = pl.DeviceIdType.MESH
BF = jnp.bfloat16
F32 = jnp.float32
R0, R1 = 32, 48
SEMS = 200


def dev(x, y, z, k):
    return ((z // 4) * 16 + y * 4 + x, (z % 4) * 2 + k)


def body(tok, up, dn, out, T, U, D, dnT, acc, H, O, Ls, Lr, S0, Q0, S1, Q1, V0, f0s, f0r, fin, finr, ss, rs):
    row = lax.axis_index("row")
    col = lax.axis_index("col")
    x, y, zh = row % 4, (row // 4) % 4, row // 16
    zl, k = col // 2, col % 2
    z = 4 * zh + zl
    hi, lo = x // 2, x % 2
    yh, yl = y // 2, y % 2
    turn = ((x + 1) // 2) % 2
    here = (x, y, z, k)
    at_core = dev(x, y, z, 1 - k)
    at_lo = dev(2 * hi + 1 - lo, y, z, k)
    at_x = dev(3 - x, y, z, k)
    at_a = dev(x, 2 * yh + 1 - yl, z, k)
    at_b = dev(x, 3 - y, z, k)
    at_z = (dev(x, y, (z + 1) % 8, k), dev(x, y, (z + 7) % 8, k))

    barrier = pltpu.get_barrier_semaphore()
    friends = [at_x, at_a, at_b, at_z[0], at_z[1]]
    for fx in (0, 1):
        for fz in (0, 1):
            for fk in (0, 1):
                if fx or fz or fk:
                    friends.append(dev(2 * hi + (1 - lo if fx else lo), y, (z + 4 * fz) % 8, 1 - k if fk else k))
    for f in friends:
        pl.semaphore_signal(barrier, inc=1, device_id=f, device_id_type=MESH)
    pl.semaphore_wait(barrier, len(friends))

    count = [0]
    pending = []

    def slots(n):
        first = count[0]
        count[0] += n
        assert count[0] <= SEMS
        return first

    def copy(src, dst, to, i, j=None):
        return pltpu.make_async_remote_copy(
            src_ref=src, dst_ref=dst, send_sem=ss.at[i], recv_sem=rs.at[i if j is None else j],
            device_id=to, device_id_type=MESH)

    def send(src, dst, to, i):
        c = copy(src, dst, to, i)
        c.start()
        pending.append(c.wait_send)
        return c

    def landed(ref, i):
        pltpu.make_async_copy(ref, ref, rs.at[i]).wait()

    lane = pl.ds(pl.multiple_of(k * 384, 128), 384)

    def spread(S, B):
        base = slots(4)
        far = zh + k - 2 * zh * k
        for g in (0, 1):
            for h in (0, 1):
                src = S.at[:, pl.ds((2 * g + h) * 384, 384)]
                dst = B.at[zh, y, x, :, pl.ds(h * 384, 384)]
                to = dev(2 * hi + (1 - hi if g else hi), y, 4 * k + zl, h)
                own = (far == 0) & (turn == g) & (k == h)

                def c(src=src, dst=dst, to=to, i=base + 2 * g + h):
                    return copy(src, dst, to, i, base + 2 * far + lo)

                @pl.when(own)
                def _():
                    pltpu.make_async_copy(src, dst, rs.at[base + 2 * far + lo]).start()

                @pl.when(jnp.logical_not(own))
                def _():
                    c().start()

                def done(own=own, c=c):
                    @pl.when(jnp.logical_not(own))
                    def _():
                        c().wait_send()
                pending.append(done)

        def arrived(zs):
            off = zs + zh - 2 * zs * zh
            for l in (0, 1):
                landed(B.at[zs, y, 2 * hi + l, :, lane], base + 2 * off + l)
        return arrived

    def gather(B, zs):
        pair, ypair = pl.ds(2 * hi, 2), pl.ds(2 * yh, 2)
        every = pl.ds(0, 4)

        def sl(ys, xs, p):
            return B.at[zs, ys, xs, pl.ds(32 * p, 32), lane]

        plan = (
            ((at_x, 0, ((y, pair),)), (at_a, 1, ((y, pair),)), (at_b, 2, ((y, pair),))),
            ((at_a, 0, ((y, every),)), (at_b, 1, ((ypair, pair),)), (at_x, 2, ((y, pair), (3 - y, pair)))),
            ((at_b, 0, ((ypair, every),)), (at_x, 1, ((every, pair),)), (at_a, 2, ((y, every), (3 - y, every)))),
        )
        live = {}

        def go(step):
            cs = []
            for to, p, sets in plan[step]:
                for ys, xs in sets:
                    r = sl(ys, xs, p)
                    cs.append(send(r, r, to, slots(1)))
            live[step] = cs

        def wait(step):
            for c in live[step]:
                c.wait_recv()

        def forward():
            r = B.at[zs, :, :, :, lane]
            live["f"] = [send(r, r, at_core, slots(1))]
        return go, wait, forward

    def t_most(st, dr):
        return 4 if st == dr else 3

    def t_slice(zo, st):
        if st == 0:
            return T.at[zo % 4, pl.ds(2 * (zo // 4), 2), pl.ds(0, R0)]
        return T.at[zo % 4, 2 * (zo // 4) + lo, pl.ds(R0, R1)]

    t_live, lo_live = {}, []

    def t_origin(dr, d):
        return (z + 8 - d) % 8 if dr == 0 else (z + d) % 8

    def t_send(st, d):
        for dr in (0, 1):
            if d <= t_most(st, dr):
                r = t_slice(t_origin(dr, d - 1), st)
                t_live[st, dr, d] = send(r, r, at_z[dr], slots(1))

    def t_wait(st, d):
        for dr in (0, 1):
            if d <= t_most(st, dr):
                t_live[st, dr, d].wait_recv()
                if st == 1:
                    t_to_lo(t_origin(dr, d))

    def t_to_lo(zo):
        r = t_slice(zo, 1)
        lo_live.append(send(r, r, at_lo, slots(1)))

    up_arrived = spread(up, U)
    q_own = 2 * zh + lo
    rows_of = lambda c: pl.ds(pl.multiple_of(c * 80, 16), 80)
    tx = slots(1)
    t_dst = T.at[zl, q_own, :, lane]
    tc = copy(tok.at[rows_of(1 - k)], t_dst, at_core, tx)
    tc.start()
    pending.append(tc.wait_send)
    i = slots(1)
    own_copy = pltpu.make_async_copy(tok.at[rows_of(k)], t_dst, rs.at[i])
    own_copy.start()

    eye = (lax.broadcasted_iota(jnp.int32, (96, 96), 0) == lax.broadcasted_iota(jnp.int32, (96, 96), 1)).astype(BF)
    dnT[...] = lax.dot_general(eye, dn[...], (((1,), (1,)), ((), ())), preferred_element_type=F32).astype(BF)

    own_copy.wait()
    tc.wait_recv()
    i = slots(1)
    r = T.at[zl, q_own, pl.ds(0, R0)]
    lo0 = send(r, r, at_lo, i)
    t_send(1, 1)
    t_to_lo(z)
    dn_arrived = spread(dnT, D)

    un, uf = gather(U, zh), gather(U, 1 - zh)
    d0, d1 = gather(D, 0), gather(D, 1)
    GO, WAIT, FWD = 0, 1, 2

    up_arrived(zh)
    un[GO](0)
    lo0.wait_recv()
    t_send(0, 1)
    un[WAIT](0)
    un[GO](1)
    t_wait(1, 1)
    t_send(1, 2)
    t_wait(0, 1)
    t_send(0, 2)
    un[WAIT](1)
    un[GO](2)
    up_arrived(1 - zh)
    uf[GO](0)
    t_wait(1, 2)
    t_send(1, 3)
    t_wait(0, 2)
    t_send(0, 3)
    uf[WAIT](0)
    uf[GO](1)
    dn_arrived(0)
    d0[GO](0)
    un[WAIT](2)
    un[FWD]()
    t_wait(1, 3)
    t_send(1, 4)
    t_wait(0, 3)
    t_send(0, 4)
    uf[WAIT](1)
    uf[GO](2)
    d0[WAIT](0)
    d0[GO](1)
    dn_arrived(1)
    d1[GO](0)
    t_wait(1, 4)
    t_wait(0, 4)
    d0[WAIT](1)
    d0[GO](2)
    d1[WAIT](0)
    uf[WAIT](2)
    uf[FWD]()
    d1[GO](1)
    for c in lo_live:
        c.wait_recv()
    un[WAIT]("f")
    uf[WAIT]("f")

    acc[...] = jnp.zeros_like(acc)

    def up_step(j, carry):
        acc[...] += jnp.dot(
            T[j].reshape(320, 768), U[j // 2, pl.ds(2 * (j % 2), 2)].reshape(768, 768), preferred_element_type=F32)
        return carry
    lax.fori_loop(0, 4, up_step, 0)

    def act(j, carry):
        r = pl.ds(pl.multiple_of(j * 32, 32), 32)
        v = acc[r, :]
        H[r, :] = (v * (1.0 + lax.erf(v * 0.7071067811865476)) * 0.5).astype(BF)
        return carry
    lax.fori_loop(0, 10, act, 0)

    def project(phi):
        for j in (0, 1):
            w = D[phi, 2 * j:2 * j + 2].reshape(768, 768)
            o = lax.dot_general(H[...], w, (((1,), (1,)), ((), ())), preferred_element_type=F32)
            O[2 * phi + j] = o.reshape(4, 80, 768)

    l_base = slots(8)
    r_base = {}
    for phi in (0, 1):
        for st in (0, 1):
            for dr in (0, 1):
                r_base[phi, st, dr] = slots(4)

    def l_copy(t):
        i = l_base + t
        return copy(Ls.at[t], Lr.at[t], at_lo, i)

    def l_send(phi):
        for off in (4, 3, 5, 2, 6, 1, 7, 0):
            t = (z + off) % 8

            @pl.when((t % 4) // 2 == phi)
            def _():
                Ls[t] = O[t % 4, 2 * (t // 4) + 1 - lo, R0:].astype(BF)
                l_copy(t).start()

            def done(t=t):
                @pl.when((t % 4) // 2 == phi)
                def _():
                    l_copy(t).wait_send()
            pending.append(done)

    def ring_copy(phi, st, dr, d):
        i = r_base[phi, st, dr] + d - 1
        S, Q = ((S0, Q0), (S1, Q1))[st]
        n = ((phi * 2 + dr) * 4) + d - 1
        return copy(S.at[n], Q.at[n], at_z[dr], i)

    def term(st, t):
        if st == 0:
            return O[t % 4, pl.ds(2 * (t // 4), 2), 0:R0]
        l_copy(t).wait_recv()
        return O[t % 4, 2 * (t // 4) + lo, R0:] + Lr[t].astype(F32)

    def ring(phi, st, d):
        for dr in (0, 1):
            if d > t_most(st, dr):
                continue
            t = (z + d) % 8 if dr == 0 else (z + 8 - d) % 8
            S, Q = ((S0, Q0), (S1, Q1))[st]

            @pl.when((t % 4) // 2 == phi)
            def _():
                v = term(st, t)
                if d < t_most(st, dr):
                    ring_copy(phi, st, dr, d + 1).wait_recv()
                    v = v + Q[(phi * 2 + dr) * 4 + d].astype(F32)
                S[(phi * 2 + dr) * 4 + d - 1] = v.astype(BF)
                ring_copy(phi, st, dr, d).start()

            def done(t=t, dr=dr):
                @pl.when((t % 4) // 2 == phi)
                def _():
                    ring_copy(phi, st, dr, d).wait_send()
            pending.append(done)

    f_i, c_i = slots(1), slots(1)

    def own_total(phi, st):
        v = term(st, z)
        Q = (Q0, Q1)[st]
        for dr in (0, 1):
            ring_copy(phi, st, dr, 1).wait_recv()
            v = v + Q[(phi * 2 + dr) * 4].astype(F32)
        return v

    f_copy = copy(f0s, f0r, at_lo, f_i)
    c_copy = copy(fin.at[1 - k], finr, at_core, c_i)

    def finish(phi):
        @pl.when((z % 4) // 2 == phi)
        def _():
            V0[...] = own_total(phi, 0)
            f0s[...] = V0[1 - lo].astype(BF)
            f_copy.start()
            w = own_total(phi, 1).astype(BF)
            fin[0, R0:] = w[:, :384]
            fin[1, R0:] = w[:, 384:]
            f_copy.wait_recv()
            w = (V0[lo] + f0r[...].astype(F32)).astype(BF)
            fin[0, 0:R0] = w[:, :384]
            fin[1, 0:R0] = w[:, 384:]
            c_copy.start()
            out[k] = fin[k]

    d0[WAIT](2)
    d0[FWD]()
    d1[WAIT](1)
    d1[GO](2)
    d0[WAIT]("f")
    project(0)
    l_send(0)
    ring(0, 0, 4)
    ring(0, 1, 4)
    ring(0, 0, 3)
    ring(0, 1, 3)
    d1[WAIT](2)
    d1[FWD]()
    ring(0, 0, 2)
    ring(0, 1, 2)
    d1[WAIT]("f")
    project(1)
    l_send(1)
    ring(1, 0, 4)
    ring(1, 1, 4)
    ring(0, 0, 1)
    ring(0, 1, 1)
    ring(1, 0, 3)
    ring(1, 1, 3)
    ring(1, 0, 2)
    ring(1, 1, 2)
    ring(1, 0, 1)
    ring(1, 1, 1)
    finish(0)
    finish(1)
    c_copy.wait_recv()
    out[1 - k] = finr[...]
    pending.append(f_copy.wait_send)
    pending.append(c_copy.wait_send)
    for w in pending:
        w()


def local(tokens, up_weight, down_weight):
    vmem = pl.BlockSpec(memory_space=pltpu.VMEM)
    out = pl.pallas_call(
        body,
        out_shape=jax.ShapeDtypeStruct((2, 80, 384), BF),
        in_specs=[vmem] * 3,
        out_specs=vmem,
        scratch_shapes=[
            pltpu.VMEM((4, 4, 80, 768), BF),
            pltpu.VMEM((2, 4, 4, 96, 768), BF),
            pltpu.VMEM((2, 4, 4, 96, 768), BF),
            pltpu.VMEM((96, 1536), BF),
            pltpu.VMEM((320, 768), F32),
            pltpu.VMEM((320, 768), BF),
            pltpu.VMEM((4, 4, 80, 768), F32),
            pltpu.VMEM((8, R1, 768), BF),
            pltpu.VMEM((8, R1, 768), BF),
            pltpu.VMEM((16, 2, R0, 768), BF),
            pltpu.VMEM((16, 2, R0, 768), BF),
            pltpu.VMEM((16, R1, 768), BF),
            pltpu.VMEM((16, R1, 768), BF),
            pltpu.VMEM((2, R0, 768), F32),
            pltpu.VMEM((R0, 768), BF),
            pltpu.VMEM((R0, 768), BF),
            pltpu.VMEM((2, 80, 384), BF),
            pltpu.VMEM((80, 384), BF),
            pltpu.SemaphoreType.DMA((SEMS,)),
            pltpu.SemaphoreType.DMA((SEMS,)),
        ],
        compiler_params=pltpu.CompilerParams(
            collective_id=0, has_side_effects=True, vmem_limit_bytes=48 << 20),
        name="ffn",
    )(tokens, up_weight, down_weight)
    return out.reshape(160, 384)


def solution(mesh):
    return jax.shard_map(
        local,
        mesh=mesh,
        in_specs=(P("row", "col"), P("row", "col"), P("col", "row")),
        out_specs=P("row", "col"),
        check_vma=False,
    )
```

```python
import jax
import jax.numpy as jnp
from jax import lax
from jax.experimental import pallas as pl
from jax.experimental.pallas import tpu as pltpu
from jax.sharding import PartitionSpec as P

MESH = pl.DeviceIdType.MESH
BF = jnp.bfloat16
F32 = jnp.float32
TA, TB = 32, 48
SEMS = 280


def dev(x, y, z, k):
    return ((z // 4) * 16 + y * 4 + x, (z % 4) * 2 + k)


def body(tok, up, dn, out, T, U, D, acc, H, O, S, Q, F, SO, OA, V, E, ss, rs):
    row = lax.axis_index("row")
    col = lax.axis_index("col")
    x, y, zh = row % 4, (row // 4) % 4, row // 16
    zl, k = col // 2, col % 2
    z = 4 * zh + zl
    hi, lo = x // 2, x % 2
    yh, yl = y // 2, y % 2
    ya = 2 * yh + 1 - yl
    turn = ((x + 1) // 2) % 2
    x_lo = 2 * hi + 1 - lo

    def ring_z(n):
        return (z + 8 + n) % 8

    at_core = dev(x, y, z, 1 - k)
    at_lo = dev(x_lo, y, z, k)
    at_x = dev(3 - x, y, z, k)
    at_a = dev(x, ya, z, k)
    at_b = dev(x, 3 - y, z, k)
    at_z = (dev(x, y, ring_z(1), k), dev(x, y, ring_z(-1), k))

    barrier = pltpu.get_barrier_semaphore()
    friends = [at_x, at_a, at_b]
    for n in (0, 4, 1, -1):
        for px in (x, x_lo):
            for pk in (k, 1 - k):
                if n or px is not x or pk is not k:
                    friends.append(dev(px, y, ring_z(n), pk))
    for f in friends:
        pl.semaphore_signal(barrier, inc=1, device_id=f, device_id_type=MESH)
    pl.semaphore_wait(barrier, len(friends))

    count = [0]
    pending = []

    def slots(n):
        first = count[0]
        count[0] += n
        assert count[0] <= SEMS
        return first

    def copy(src, dst, to, i, j=None):
        return pltpu.make_async_remote_copy(
            src_ref=src, dst_ref=dst, send_sem=ss.at[i], recv_sem=rs.at[i if j is None else j],
            device_id=to, device_id_type=MESH)

    def send(src, dst, to, i=None, j=None):
        c = copy(src, dst, to, slots(1) if i is None else i, j)
        c.start()
        pending.append(c.wait_send)
        return c

    def landed(ref, i):
        pltpu.make_async_copy(ref, ref, rs.at[i]).wait()

    def spread(S, at):
        base = slots(4)
        far = zh + k - 2 * zh * k
        for g in (0, 1):
            for h in (0, 1):
                src = S.at[..., pl.ds((2 * g + h) * 384, 384)]
                dst = at(h, zh, x)
                to = dev(2 * hi + (1 - hi if g else hi), y, 4 * k + zl, h)
                own = (far == 0) & (turn == g) & (k == h)

                def c(src=src, dst=dst, to=to, i=base + 2 * g + h):
                    return copy(src, dst, to, i, base + 2 * far + lo)

                @pl.when(own)
                def _():
                    pltpu.make_async_copy(src, dst, rs.at[base + 2 * far + lo]).start()

                @pl.when(jnp.logical_not(own))
                def _():
                    c().start()

                def done(own=own, c=c):
                    @pl.when(jnp.logical_not(own))
                    def _():
                        c().wait_send()
                pending.append(done)

        def arrived(zs):
            off = zs + zh - 2 * zs * zh
            for l in (0, 1):
                landed(at(k, zs, 2 * hi + l), base + 2 * off + l)
        return arrived

    pair, other = pl.ds(2 * hi, 2), pl.ds(2 - 2 * hi, 2)
    ypair, yother = pl.ds(2 * yh, 2), pl.ds(2 - 2 * yh, 2)
    every = pl.ds(0, 4)
    plan = (
        ((at_x, 0, ((y, pair),)), (at_a, 1, ((y, pair),)), (at_b, 2, ((y, pair),))),
        ((at_a, 0, ((y, every),)), (at_b, 1, ((ypair, pair),)), (at_x, 2, ((y, pair), (3 - y, pair)))),
        ((at_b, 0, ((ypair, every),)), (at_x, 1, ((every, pair),)), (at_a, 2, ((y, every), (3 - y, every)))),
    )
    held = tuple((p, s) for _, p, s in plan[2])
    last = ((0, ((yother, every),)), (1, ((every, other),)), (2, ((ya, every), (3 - ya, every))))

    class Gather:
        def __init__(self, part):
            self.part, self.live = part, {}

        def go(self, step):
            rs_ = [(to, self.part(ys, xs, p)) for to, p, sets in plan[step] for ys, xs in sets]
            self.live[step] = [send(r, r, to) for to, r in rs_]

        def wait(self, step):
            for c in self.live[step]:
                c.wait_recv()

        def forward(self, what):
            rs_ = [self.part(ys, xs, p) for p, sets in what for ys, xs in sets]
            self.live["f"] = self.live.get("f", []) + [send(r, r, at_core) for r in rs_]

    def up_part(zs):
        return lambda ys, xs, p: U.at[k, zs, ys, xs, pl.ds(32 * p, 32)]

    def dn_part(zs):
        return lambda ys, xs, p: D.at[:, k, zs, ys, xs, :, pl.ds(128 * p, 128)]

    def dn_last(b):
        return lambda ys, xs, p: D.at[b, k, :, ys, xs, :, pl.ds(128 * p, 128)]

    def most(st, dr):
        return 4 if st == dr else 3

    def t_slice(zo, st):
        if st == 0:
            return T.at[zo % 4, pl.ds(2 * (zo // 4), 2), pl.ds(0, TA)]
        return T.at[zo % 4, 2 * (zo // 4) + lo, pl.ds(TA, TB)]

    t_live, lo_live = {}, []

    def t_origin(dr, d):
        return ring_z(-d if dr == 0 else d)

    def t_send(st, d):
        for dr in (0, 1):
            if d <= most(st, dr):
                r = t_slice(t_origin(dr, d - 1), st)
                t_live[st, dr, d] = send(r, r, at_z[dr])

    def t_wait(st, d):
        for dr in (0, 1):
            if d <= most(st, dr):
                t_live[st, dr, d].wait_recv()
                if st == 1:
                    t_to_lo(t_origin(dr, d))

    def t_to_lo(zo):
        r = t_slice(zo, 1)
        lo_live.append(send(r, r, at_lo))

    def project(b):
        w = jnp.concatenate([D[b, h].reshape(1024, 384) for h in (0, 1)], axis=1)
        o = lax.dot_general(H[...], w, (((1,), (1,)), ((), ())), preferred_element_type=F32)
        for j in range(8):
            O[b, j // 2, j % 2] = o[:, 128 * j:128 * j + 128].reshape(4, 80, 128)

    ring_base = slots(24)
    last_send, last_recv = slots(24), slots(24)
    own_send, own_recv = slots(9), slots(12)

    def far_dir(b, dr):
        return b % 2 == dr

    def ring_copies(b, dr, d):
        n = (b * 2 + dr) * 4
        src = S.at[n + d - 1]
        if d > 1:
            return [copy(src, Q.at[n + d - 1], at_z[dr], ring_base + n + d - 1)]
        zt = ring_z(1 if dr == 0 else -1)
        return [copy(src.at[c, l], F.at[b, dr, k, lo], dev(2 * hi + l, y, zt, c),
                     last_send + n + 2 * c + l, last_recv + n + 2 * k + lo)
                for c in (0, 1) for l in (0, 1)]

    def ring(b, step):
        for dr in (0, 1):
            first = 4 if far_dir(b, dr) else 3
            d = first - step
            if d == 0:
                continue
            t = ring_z(d if dr == 0 else -d)
            n = (b * 2 + dr) * 4
            v = O[b, t % 4, :, pl.ds(2 * (t // 4), 2)]
            if step:
                ring_copies(b, dr, d + 1)[0].wait_recv()
                v = v + Q[n + d].astype(F32)
            S[n + d - 1] = v.astype(BF)
            for c in ring_copies(b, dr, d):
                c.start()
                pending.append(c.wait_send)

    def own(b):
        SO[b] = O[b, zl, :, pl.ds(2 * zh, 2)].astype(BF)
        for i, (l, c) in enumerate(((lo, 1 - k), (1 - lo, k), (1 - lo, 1 - k))):
            send(SO.at[b, c, l], OA.at[b, k, lo], dev(2 * hi + l, y, z, c), own_send + 3 * b + i, own_recv + 4 * b + 2 * k + lo)

    def up32(r):
        return r.astype(F32)

    def finish(b):
        for l in (0, 1):
            landed(OA.at[b, 1 - k, l], own_recv + 4 * b + 2 * (1 - k) + l)
        landed(OA.at[b, k, 1 - lo], own_recv + 4 * b + 2 * k + 1 - lo)
        for kk in (1 - k, k):
            if kk is k:
                v = O[b, zl, k, 2 * zh + lo] + up32(OA[b, k, 1 - lo])
            else:
                v = up32(OA[b, kk, 0]) + up32(OA[b, kk, 1])
            for dr in (0, 1):
                for l in (0, 1):
                    landed(F.at[b, dr, kk, l], last_recv + (b * 2 + dr) * 4 + 2 * kk + l)
                    v = v + up32(F[b, dr, kk, l])
            V[kk, :, 128 * b:128 * b + 128] = v.astype(BF)

    def order():
        i = lax.broadcasted_iota(jnp.int32, (384, 384), 0)
        j = lax.broadcasted_iota(jnp.int32, (384, 384), 1)
        E[...] = (j == 96 * ((i % 128) // 32) + 32 * (i // 128) + i % 32).astype(F32).astype(BF)

    def pre():
        for h in (0, 1):
            v = None
            for j in range(4):
                o = jnp.dot(T[j].reshape(320, 768), U[h, j // 2, 2 * (j % 2):2 * (j % 2) + 2].reshape(768, 384),
                            preferred_element_type=F32)
                v = o if v is None else v + o
            acc[h] = v

    def act(j, carry):
        r = pl.ds(pl.multiple_of(j * 80, 16), 80)
        for h in (0, 1):
            v = acc[h, r, :]
            H[r, h * 384:(h + 1) * 384] = (v * (1.0 + lax.erf(v * 0.7071067811865476)) * 0.5).astype(BF)
        return carry

    up_arrived = spread(up, lambda h, zs, xs: U.at[h, zs, y, xs])

    def rows_of(c):
        return pl.ds(pl.multiple_of(c * 80, 16), 80)

    lane = pl.ds(pl.multiple_of(k * 384, 128), 384)
    q_own = 2 * zh + lo
    t_dst = T.at[zl, q_own, :, lane]
    tc = send(tok.at[rows_of(1 - k)], t_dst, at_core)
    own_copy = pltpu.make_async_copy(tok.at[rows_of(k)], t_dst, rs.at[slots(1)])
    own_copy.start()
    dn_arrived = spread(dn, lambda h, zs, xs: D.at[:, h, zs, y, xs])

    un, uf = Gather(up_part(zh)), Gather(up_part(1 - zh))
    dN, dF = Gather(dn_part(zh)), Gather(dn_part(1 - zh))
    d0, d1, d2 = Gather(dn_last(0)), Gather(dn_last(1)), Gather(dn_last(2))

    own_copy.wait()
    tc.wait_recv()
    t_send(1, 1)
    r = T.at[zl, q_own, pl.ds(0, TA)]
    lo0 = send(r, r, at_lo)
    t_to_lo(z)
    up_arrived(zh)
    un.go(0)
    dn_arrived(zh)
    dN.go(0)
    lo0.wait_recv()
    t_send(0, 1)
    order()
    un.wait(0)
    un.go(1)
    dN.wait(0)
    dN.go(1)
    up_arrived(1 - zh)
    uf.go(0)
    un.wait(1)
    un.go(2)
    un.forward(held)
    uf.wait(0)
    uf.go(1)
    dn_arrived(1 - zh)
    dF.go(0)
    t_wait(1, 1)
    t_send(1, 2)
    t_wait(0, 1)
    t_send(0, 2)
    un.wait(2)
    un.forward(last)
    uf.wait(1)
    uf.go(2)
    uf.forward(held)
    t_wait(1, 2)
    t_send(1, 3)
    dN.wait(1)
    dF.wait(0)
    dF.go(1)
    t_wait(0, 2)
    t_send(0, 3)
    t_wait(1, 3)
    t_send(1, 4)
    t_wait(0, 3)
    t_send(0, 4)
    uf.wait(2)
    uf.forward(last)
    dF.wait(1)
    d0.go(2)
    d1.go(2)
    d2.go(2)
    d0.forward(held)
    d1.forward(held)
    d2.forward(held)
    t_wait(1, 4)
    t_wait(0, 4)
    for c in lo_live:
        c.wait_recv()
    un.wait("f")
    uf.wait("f")
    pre()
    lax.fori_loop(0, 4, act, 0)
    d0.wait(2)
    d0.forward(last)
    d1.wait(2)
    d1.forward(last)
    d0.wait("f")
    project(0)
    ring(0, 0)
    own(0)
    d2.wait(2)
    d2.forward(last)
    d1.wait("f")
    project(1)
    ring(1, 0)
    own(1)
    ring(0, 1)
    d2.wait("f")
    project(2)
    ring(2, 0)
    own(2)
    ring(1, 1)
    ring(0, 2)
    ring(2, 1)
    ring(1, 2)
    ring(0, 3)
    ring(2, 2)
    ring(1, 3)
    finish(0)
    ring(2, 3)
    finish(1)
    finish(2)
    out[...] = jnp.dot(V[...].reshape(160, 384), E[...], preferred_element_type=F32).astype(BF)
    for w in pending:
        w()


def local(tokens, up_weight, down_weight):
    vmem = pl.BlockSpec(memory_space=pltpu.VMEM)
    hbm = pl.BlockSpec(memory_space=pltpu.HBM)
    out = pl.pallas_call(
        body,
        out_shape=jax.ShapeDtypeStruct((160, 384), BF),
        in_specs=[hbm] * 3,
        out_specs=vmem,
        scratch_shapes=[
            pltpu.VMEM((4, 4, 80, 768), BF),
            pltpu.VMEM((2, 2, 4, 4, 96, 384), BF),
            pltpu.VMEM((3, 2, 2, 4, 4, 32, 384), BF),
            pltpu.VMEM((2, 320, 384), F32),
            pltpu.VMEM((320, 768), BF),
            pltpu.VMEM((3, 4, 2, 4, 80, 128), F32),
            pltpu.VMEM((24, 2, 2, 80, 128), BF),
            pltpu.VMEM((24, 2, 2, 80, 128), BF),
            pltpu.VMEM((3, 2, 2, 2, 80, 128), BF),
            pltpu.VMEM((3, 2, 2, 80, 128), BF),
            pltpu.VMEM((3, 2, 2, 80, 128), BF),
            pltpu.VMEM((2, 80, 384), BF),
            pltpu.VMEM((384, 384), BF),
            pltpu.SemaphoreType.DMA((SEMS,)),
            pltpu.SemaphoreType.DMA((SEMS,)),
        ],
        compiler_params=pltpu.CompilerParams(
            collective_id=0, has_side_effects=True, vmem_limit_bytes=63 << 20),
        name="ffn",
    )(tokens, up_weight, down_weight.T.reshape(3, 32, 1536))
    return out


def solution(mesh):
    return jax.shard_map(
        local,
        mesh=mesh,
        in_specs=(P("row", "col"), P("row", "col"), P("col", "row")),
        out_specs=P("row", "col"),
        check_vma=False,
    )
```

```python
import jax
import jax.numpy as jnp
from jax import lax
from jax.experimental import pallas as pl
from jax.experimental.pallas import tpu as pltpu
from jax.sharding import PartitionSpec as P

MESH = pl.DeviceIdType.MESH
BF = jnp.bfloat16
F32 = jnp.float32
TA, TB = 32, 48
RA, RB = 80, 0
SEMS = 460
ORDER = (
    "uS1", "Tc", "uS0", "T11", "dS1", "un1", "dn11", "T0lo",
    "uf11", "un2", "uf01", "uf12", "dn12", "T01", "un3", "T12",
    "dS0", "df11", "Tl1", "uf1h", "Tl0", "dn01", "T02", "uf02",
    "unh", "uf13", "Tl2", "T13", "df01", "df12", "dn02", "T03",
    "T14", "uf03", "Tl3", "df02", "dn23x", "unl", "T04", "df23x",
    "uf1l", "dn03x", "Tl4", "uf0l", "df03x", "df13x", "uf0h", "dh0",
    "dn13x", "dl2", "dh1", "qre", "pre", "dl0", "p2", "r20",
    "dl1", "p0", "r00", "p1", "r10", "r21", "r01", "r11",
    "r22", "r02", "r12", "r23", "r03", "r13", "f2", "f0",
    "f1",
)


def dev(x, y, z, k):
    return ((z // 4) * 16 + y * 4 + x, (z % 4) * 2 + k)


def body(tok_h, up_h, dn_h, out, tok, up, dn, T, U, D, acc, H, O, SA, QA, FA, SO, OA, V, E, ss, rs, ls):
    row = lax.axis_index("row")
    col = lax.axis_index("col")
    x, y, zh = row % 4, (row // 4) % 4, row // 16
    zl, k = col // 2, col % 2
    z = 4 * zh + zl
    hi, lo = x // 2, x % 2
    yh, yl = y // 2, y % 2
    ya = 2 * yh + 1 - yl
    turn = ((x + 1) // 2) % 2
    x_lo = 2 * hi + 1 - lo

    def ring_z(n):
        return (z + 8 + n) % 8

    at_core = dev(x, y, z, 1 - k)
    at_lo = dev(x_lo, y, z, k)
    at_x = dev(3 - x, y, z, k)
    at_a = dev(x, ya, z, k)
    at_b = dev(x, 3 - y, z, k)
    at_z = (dev(x, y, ring_z(1), k), dev(x, y, ring_z(-1), k))

    loads = [pltpu.make_async_copy(a, b, ls.at[i]) for i, (a, b) in enumerate(((up_h, up), (tok_h, tok), (dn_h, dn)))]
    for c in loads:
        c.start()
    barrier = pltpu.get_barrier_semaphore()
    friends = [at_x, at_a, at_b]
    for n in (0, 4, 1, -1):
        for px in (x, x_lo):
            for pk in (k, 1 - k):
                if n or px is not x or pk is not k:
                    friends.append(dev(px, y, ring_z(n), pk))
    for f in friends:
        pl.semaphore_signal(barrier, inc=1, device_id=f, device_id_type=MESH)
    pl.semaphore_wait(barrier, len(friends))
    for c in loads:
        c.wait()

    count = [0]
    pending = []

    def slots(n):
        first = count[0]
        count[0] += n
        assert count[0] <= SEMS
        return first

    def copy(src, dst, to, i, j=None):
        return pltpu.make_async_remote_copy(
            src_ref=src, dst_ref=dst, send_sem=ss.at[i], recv_sem=rs.at[i if j is None else j],
            device_id=to, device_id_type=MESH)

    def send(src, dst, to, i=None, j=None):
        c = copy(src, dst, to, slots(1) if i is None else i, j)
        c.start()
        pending.append(c.wait_send)
        return c

    def landed(ref, i):
        pltpu.make_async_copy(ref, ref, rs.at[i]).wait()

    def spread(S, at):
        base = slots(4)
        far = zh + k - 2 * zh * k
        for g in (0, 1):
            for h in (0, 1):
                src = S.at[..., pl.ds((2 * g + h) * 384, 384)]
                dst = at(h, zh, x)
                to = dev(2 * hi + (1 - hi if g else hi), y, 4 * k + zl, h)
                own = (far == 0) & (turn == g) & (k == h)

                def c(src=src, dst=dst, to=to, i=base + 2 * g + h):
                    return copy(src, dst, to, i, base + 2 * far + lo)

                @pl.when(own)
                def _():
                    pltpu.make_async_copy(src, dst, rs.at[base + 2 * far + lo]).start()

                @pl.when(jnp.logical_not(own))
                def _():
                    c().start()

                def done(own=own, c=c):
                    @pl.when(jnp.logical_not(own))
                    def _():
                        c().wait_send()
                pending.append(done)

        def arrived(zs):
            off = zs + zh - 2 * zs * zh
            for l in (0, 1):
                landed(at(k, zs, 2 * hi + l), base + 2 * off + l)
        return arrived

    pair, other = pl.ds(2 * hi, 2), pl.ds(2 - 2 * hi, 2)
    ypair, yother = pl.ds(2 * yh, 2), pl.ds(2 - 2 * yh, 2)
    every = pl.ds(0, 4)
    plan = (
        ((at_x, 0, ((y, pair),)), (at_a, 1, ((y, pair),)), (at_b, 2, ((y, pair),))),
        ((at_a, 0, ((y, every),)), (at_b, 1, ((ypair, pair),)), (at_x, 2, ((y, pair), (3 - y, pair)))),
        ((at_b, 0, ((ypair, every),)), (at_x, 1, ((every, pair),)), (at_a, 2, ((y, every), (3 - y, every)))),
    )
    held = tuple((p, s) for _, p, s in plan[2])
    last = ((0, ((yother, every),)), (1, ((every, other),)), (2, ((ya, every), (3 - ya, every))))

    class Gather:
        def __init__(self, part):
            self.part, self.live = part, {}

        def go(self, step):
            rs_ = [(to, self.part(ys, xs, p)) for to, p, sets in plan[step] for ys, xs in sets]
            self.live[step] = [send(r, r, to) for to, r in rs_]

        def wait(self, step):
            for c in self.live.pop(step, ()):
                c.wait_recv()

        def forward(self, what):
            rs_ = [self.part(ys, xs, p) for p, sets in what for ys, xs in sets]
            self.live["f"] = self.live.get("f", []) + [send(r, r, at_core) for r in rs_]

    def up_part(zs, rows=slice(None)):
        return lambda ys, xs, p: U.at[k, zs, ys, xs, p, rows]

    phases = (0, pl.ds(1, 2))

    def dn_part(g, zs):
        return lambda ys, xs, p: D.at[phases[g], k, zs, ys, xs, :, pl.ds(128 * p, 128)]

    def dn_last(b, zs):
        return lambda ys, xs, p: D.at[b, k, zs, ys, xs, :, pl.ds(128 * p, 128)]

    def most(st, dr):
        return 4 if st == dr else 3

    def t_slice(zo, st):
        if st == 0:
            return T.at[zo % 4, pl.ds(2 * (zo // 4), 2), pl.ds(0, TA)]
        return T.at[zo % 4, 2 * (zo // 4) + lo, pl.ds(TA, TB)]

    sent, lo_live, seen = {}, [], set()

    def need(*name):
        if name not in seen:
            seen.add(name)
            sent[name].wait_recv()

    def t_origin(dr, d):
        return ring_z(-d if dr == 0 else d)

    def t_send(st, d):
        for dr in (0, 1):
            if d <= most(st, dr):
                if d > 1:
                    need("t", st, dr, d - 1)
                r = t_slice(t_origin(dr, d - 1), st)
                sent["t", st, dr, d] = send(r, r, at_z[dr])

    def t_lo(d):
        for dr in (0, 1):
            if d <= most(1, dr):
                need("t", 1, dr, d)
                t_to_lo(t_origin(dr, d))

    def t_to_lo(zo):
        r = t_slice(zo, 1)
        lo_live.append(send(r, r, at_lo))

    def project(b):
        w = jnp.concatenate([D[b, h].reshape(1024, 384) for h in (0, 1)], axis=1)
        o = lax.dot_general(H[...], w, (((1,), (1,)), ((), ())), preferred_element_type=F32)
        for j in range(8):
            O[b, j // 2, j % 2] = o[:, 128 * j:128 * j + 128].reshape(4, 80, 128)

    ring_base = slots(48)
    last_send, last_recv = slots(36), slots(36)
    own_send, own_recv = slots(12), slots(15)
    l_base = slots(24)
    cut = (slice(0, RA), slice(RA, 80))

    def far_dir(b, st, dr):
        return (b + st) % 2 == dr

    def term(b, st, t):
        return O[b, t % 4, :, pl.ds(2 * (t // 4), 2)]

    def ring_copies(b, st, dr, d):
        m = (b * 2 + dr) * 4
        S, Q = SA, QA
        src, i = S.at[m + d - 1], ring_base + 24 * st + m
        if d > 1:
            return [copy(src, Q.at[m + d - 1], at_z[dr], i + d - 1)]
        zt = ring_z(1 if dr == 0 else -1)
        if True:
            return [copy(src.at[c, l], FA.at[b, dr, k, lo], dev(2 * hi + l, y, zt, c),
                         last_send + m + 2 * c + l, last_recv + m + 2 * k + lo)
                    for c in (0, 1) for l in (0, 1)]

    def ring(b, st, step):
        S, Q = SA, QA
        for dr in (0, 1):
            d = (4 if far_dir(b, st, dr) else 3) - step
            if d == 0:
                continue
            m = (b * 2 + dr) * 4
            v = term(b, st, ring_z(d if dr == 0 else -d))
            if step:
                ring_copies(b, st, dr, d + 1)[0].wait_recv()
                v = v + Q[m + d].astype(F32)
            S[m + d - 1] = v.astype(BF)
            for c in ring_copies(b, st, dr, d):
                c.start()
                pending.append(c.wait_send)

    def own(b):
        SO[b] = O[b, zl, :, pl.ds(2 * zh, 2), 0:RA].astype(BF)
        for i, (l, c) in enumerate(((lo, 1 - k), (1 - lo, k), (1 - lo, 1 - k))):
            send(SO.at[b, c, l], OA.at[b, k, lo], dev(2 * hi + l, y, z, c), own_send + 4 * b + i, own_recv + 5 * b + 2 * k + lo)

    def up32(r):
        return r.astype(F32)

    def finish(b):
        for l in (0, 1):
            landed(OA.at[b, 1 - k, l], own_recv + 5 * b + 2 * (1 - k) + l)
        landed(OA.at[b, k, 1 - lo], own_recv + 5 * b + 2 * k + 1 - lo)
        for kk in (1 - k, k):
            if kk is k:
                v = O[b, zl, k, 2 * zh + lo, 0:RA] + up32(OA[b, k, 1 - lo])
            else:
                v = up32(OA[b, kk, 0]) + up32(OA[b, kk, 1])
            for dr in (0, 1):
                for l in (0, 1):
                    landed(FA.at[b, dr, kk, l], last_recv + (b * 2 + dr) * 4 + 2 * kk + l)
                    v = v + up32(FA[b, dr, kk, l])
            V[kk, 0:RA, 128 * b:128 * b + 128] = v.astype(BF)

    def order():
        i = lax.broadcasted_iota(jnp.int32, (384, 384), 0)
        j = lax.broadcasted_iota(jnp.int32, (384, 384), 1)
        E[...] = (j == 96 * ((i % 128) // 32) + 32 * (i // 128) + i % 32).astype(F32).astype(BF)

    def pre(zs, first):
        for h in (0, 1):
            v = None if first else acc[h]
            for j in (0, 1):
                o = jnp.dot(T[2 * zs + j].reshape(320, 768), U[h, zs, 2 * j:2 * j + 2].reshape(768, 384),
                            preferred_element_type=F32)
                v = o if v is None else v + o
            acc[h] = v

    def act(j, carry):
        r = pl.ds(pl.multiple_of(j * 80, 16), 80)
        for h in (0, 1):
            v = acc[h, r, :]
            H[r, h * 384:(h + 1) * 384] = (v * (1.0 + lax.erf(v * 0.7071067811865476)) * 0.5).astype(BF)
        return carry

    rows_of = lambda c: pl.ds(pl.multiple_of(c * 80, 16), 80)
    lane = pl.ds(pl.multiple_of(k * 384, 128), 384)
    q_own = 2 * zh + lo
    t_dst = T.at[zl, q_own, :, lane]
    own_copy = pltpu.make_async_copy(tok.at[rows_of(k)], t_dst, rs.at[slots(1)])
    arrived = {}
    halves = (pl.ds(0, 16), pl.ds(16, 16))
    un = Gather(up_part(zh))
    uf = [Gather(up_part(1 - zh, r)) for r in halves]
    dn_g = [Gather(dn_part(g, zh)) for g in (0, 1)]
    df_g = [Gather(dn_part(g, 1 - zh)) for g in (0, 1)]
    dh_g = [Gather(dn_part(g, pl.ds(0, 2))) for g in (0, 1)]
    near = [Gather(dn_last(b, zh)) for b in range(3)]
    far = [Gather(dn_last(b, 1 - zh)) for b in range(3)]
    both = [Gather(dn_last(b, pl.ds(0, 2))) for b in range(3)]

    def ready(what, zs):
        if (what, zs is zh) not in seen:
            seen.add((what, zs is zh))
            arrived[what](zs)

    def tokens_in():
        sent["tc",] = send(tok.at[rows_of(1 - k)], t_dst, at_core)
        own_copy.start()

    def tokens_here():
        if "own" not in seen:
            seen.add("own")
            own_copy.wait()
        need("tc")

    def gather_step(G, what, zs, step):
        if step == 0:
            ready(what, zs)
        else:
            G.wait(step - 1)
        G.go(step)

    def tokens_all():
        if "all" not in seen:
            seen.add("all")
            for c in lo_live:
                c.wait_recv()
            for dr in (0, 1):
                need("t", 0, dr, most(0, dr))

    def hidden():
        for G in uf:
            G.wait("f")
        pre(1 - zh, False)
        lax.fori_loop(0, 4, act, 0)

    def run(op):
        kind, n = op[0], op[1:]
        if op[:2] == "uS":
            i = int(op[2])
            arrived["u", i] = spread(up.at[:, halves[i]], lambda h, zs, xs: U.at[h, zs, y, xs, :, halves[i]])
        elif op == "Tc":
            tokens_in()
        elif op == "T0lo":
            tokens_here()
            r = T.at[zl, q_own, pl.ds(0, TA)]
            sent["lo",] = send(r, r, at_lo)
        elif op == "Tl0":
            tokens_here()
            t_to_lo(z)
        elif op[:2] == "Tl":
            t_lo(int(op[2]))
        elif kind == "T":
            if op == "T01":
                need("lo")
            if op == "T11":
                tokens_here()
            t_send(int(op[1]), int(op[2]))
        elif op[:2] == "dS":
            g = int(op[2])
            arrived["d", g] = spread(dn.at[phases[g]], lambda h, zs, xs: D.at[phases[g], h, zs, y, xs])
        elif kind == "u":
            i = 0 if op[1] == "n" else int(op[2])
            G, zs, what = (un, zh, op[2:]) if op[1] == "n" else (uf[i], 1 - zh, op[3:])
            if what == "h":
                G.wait(1)
                G.forward(held)
            elif what == "l":
                G.wait(2)
                G.forward(last)
            else:
                if what == "1":
                    for j in ((0, 1) if op[1] == "n" else (i,)):
                        ready(("u", j), zs)
                else:
                    G.wait(int(what) - 2)
                G.go(int(what) - 1)
        elif op == "qre":
            tokens_all()
            un.wait("f")
            pre(zh, True)
        elif op[:2] == "dh":
            g = int(op[2])
            dn_g[g].wait(1)
            df_g[g].wait(1)
            dh_g[g].forward(held)
        elif op[:2] == "dl":
            b = int(op[2])
            near[b].wait(2)
            far[b].wait(2)
            both[b].forward(last)
        elif kind == "d":
            i = int(op[2])
            G, zs, L = (dn_g, zh, near) if op[1] == "n" else (df_g, 1 - zh, far)
            if op[3:] == "3x":
                G[min(i, 1)].wait(1)
                L[i].go(2)
            else:
                gather_step(G[i], ("d", i), zs, int(op[3]) - 1)
        elif op == "pre":
            hidden()
        elif kind == "p":
            b = int(n)
            dh_g[min(b, 1)].wait("f")
            both[b].wait("f")
            project(b)
        elif kind == "r":
            ring(int(n[0]), 0, int(n[1]))
            if n[1] == "0":
                own(int(n[0]))
        elif kind == "f":
            finish(int(n))

    for op in ORDER:
        if op == "un1":
            order()
        run(op)
    out[...] = jnp.dot(V[...].reshape(160, 384), E[...], preferred_element_type=F32).astype(BF)
    for w in pending:
        w()


def local(tokens, up_weight, down_weight):
    vmem = pl.BlockSpec(memory_space=pltpu.VMEM)
    hbm = pl.BlockSpec(memory_space=pltpu.HBM)
    out = pl.pallas_call(
        body,
        out_shape=jax.ShapeDtypeStruct((160, 384), BF),
        in_specs=[hbm] * 3,
        out_specs=vmem,
        scratch_shapes=[
            pltpu.VMEM((160, 384), BF),
            pltpu.VMEM((3, 32, 1536), BF),
            pltpu.VMEM((3, 32, 1536), BF),
            pltpu.VMEM((4, 4, 80, 768), BF),
            pltpu.VMEM((2, 2, 4, 4, 3, 32, 384), BF),
            pltpu.VMEM((3, 2, 2, 4, 4, 32, 384), BF),
            pltpu.VMEM((2, 320, 384), F32),
            pltpu.VMEM((320, 768), BF),
            pltpu.VMEM((3, 4, 2, 4, 80, 128), F32),
            pltpu.VMEM((24, 2, 2, RA, 128), BF),
            pltpu.VMEM((24, 2, 2, RA, 128), BF),
            pltpu.VMEM((3, 2, 2, 2, RA, 128), BF),
            pltpu.VMEM((3, 2, 2, RA, 128), BF),
            pltpu.VMEM((3, 2, 2, RA, 128), BF),
            pltpu.VMEM((2, 80, 384), BF),
            pltpu.VMEM((384, 384), BF),
            pltpu.SemaphoreType.DMA((SEMS,)),
            pltpu.SemaphoreType.DMA((SEMS,)),
            pltpu.SemaphoreType.DMA((3,)),
        ],
        compiler_params=pltpu.CompilerParams(
            collective_id=0, has_side_effects=True, vmem_limit_bytes=55040 << 10),
        name="ffn",
    )(tokens, up_weight.reshape(3, 32, 1536), down_weight.T.reshape(3, 32, 1536))
    return out


def solution(mesh):
    return jax.shard_map(
        local,
        mesh=mesh,
        in_specs=(P("row", "col"), P("row", "col"), P("col", "row")),
        out_specs=P("row", "col"),
        check_vma=False,
    )
```

```python
import jax
import jax.numpy as jnp
from jax import lax
from jax.experimental import pallas as pl
from jax.experimental.pallas import tpu as pltpu
from jax.sharding import PartitionSpec as P

MESH = pl.DeviceIdType.MESH
BF = jnp.bfloat16
F32 = jnp.float32
TA, TB = 32, 48
RA, RB = 80, 0
SEMS = 460
ORDER = (
    "uS1", "Tc", "uS0", "T11", "dS1", "un1", "dn11", "T0lo",
    "uf11", "un2", "uf01", "uf12", "dn12", "T01", "un3", "T12",
    "dS0", "df11", "Tl1", "uf1h", "Tl0", "dn01", "T02", "uf02",
    "unh", "uf13", "Tl2", "T13", "df01", "df12", "dn02", "T03",
    "T14", "uf03", "Tl3", "df02", "dn23x", "unl", "T04", "df23x",
    "uf1l", "dn03x", "Tl4", "uf0l", "df03x", "df13x", "uf0h", "dh0",
    "dn13x", "dl2", "dh1", "qre", "pre", "dl0", "p2", "r20",
    "dl1", "p0", "r00", "p1", "r10", "r21", "r01", "r11",
    "r22", "r02", "r12", "r23", "r03", "r13", "f2", "f0",
    "f1",
)


def dev(x, y, z, k):
    return ((z // 4) * 16 + y * 4 + x, (z % 4) * 2 + k)


def body(tok_h, up_h, dn_h, out, tok, up, dn, T, U, D, acc, H, O, SA, QA, FA, SO, OA, V, E, ss, rs, ls):
    row = lax.axis_index("row")
    col = lax.axis_index("col")
    x, y, zh = row % 4, (row // 4) % 4, row // 16
    zl, k = col // 2, col % 2
    z = 4 * zh + zl
    hi, lo = x // 2, x % 2
    yh, yl = y // 2, y % 2
    ya = 2 * yh + 1 - yl
    turn = ((x + 1) // 2) % 2
    x_lo = 2 * hi + 1 - lo

    def ring_z(n):
        return (z + 8 + n) % 8

    at_core = dev(x, y, z, 1 - k)
    at_lo = dev(x_lo, y, z, k)
    at_x = dev(3 - x, y, z, k)
    at_a = dev(x, ya, z, k)
    at_b = dev(x, 3 - y, z, k)
    at_z = (dev(x, y, ring_z(1), k), dev(x, y, ring_z(-1), k))

    loads = [pltpu.make_async_copy(a, b, ls.at[i]) for i, (a, b) in enumerate(((up_h, up), (tok_h, tok), (dn_h, dn)))]
    for c in loads:
        c.start()
    barrier = pltpu.get_barrier_semaphore()
    friends = [at_x, at_a, at_b]
    for n in (0, 4, 1, -1):
        for px in (x, x_lo):
            for pk in (k, 1 - k):
                if n or px is not x or pk is not k:
                    friends.append(dev(px, y, ring_z(n), pk))
    for f in friends:
        pl.semaphore_signal(barrier, inc=1, device_id=f, device_id_type=MESH)
    pl.semaphore_wait(barrier, len(friends))
    for c in loads:
        c.wait()

    count = [0]
    pending = []

    def slots(n):
        first = count[0]
        count[0] += n
        assert count[0] <= SEMS
        return first

    def copy(src, dst, to, i, j=None):
        return pltpu.make_async_remote_copy(
            src_ref=src, dst_ref=dst, send_sem=ss.at[i], recv_sem=rs.at[i if j is None else j],
            device_id=to, device_id_type=MESH)

    def send(src, dst, to, i=None, j=None):
        c = copy(src, dst, to, slots(1) if i is None else i, j)
        c.start()
        pending.append(c.wait_send)
        return c

    def landed(ref, i):
        pltpu.make_async_copy(ref, ref, rs.at[i]).wait()

    def spread(S, at):
        base = slots(4)
        far = zh + k - 2 * zh * k
        for g in (0, 1):
            for h in (0, 1):
                src = S.at[..., pl.ds((2 * g + h) * 384, 384)]
                dst = at(h, zh, x)
                to = dev(2 * hi + (1 - hi if g else hi), y, 4 * k + zl, h)
                own = (far == 0) & (turn == g) & (k == h)

                def c(src=src, dst=dst, to=to, i=base + 2 * g + h):
                    return copy(src, dst, to, i, base + 2 * far + lo)

                @pl.when(own)
                def _():
                    pltpu.make_async_copy(src, dst, rs.at[base + 2 * far + lo]).start()

                @pl.when(jnp.logical_not(own))
                def _():
                    c().start()

                def done(own=own, c=c):
                    @pl.when(jnp.logical_not(own))
                    def _():
                        c().wait_send()
                pending.append(done)

        def arrived(zs):
            off = zs + zh - 2 * zs * zh
            for l in (0, 1):
                landed(at(k, zs, 2 * hi + l), base + 2 * off + l)
        return arrived

    pair, other = pl.ds(2 * hi, 2), pl.ds(2 - 2 * hi, 2)
    ypair, yother = pl.ds(2 * yh, 2), pl.ds(2 - 2 * yh, 2)
    every = pl.ds(0, 4)
    plan = (
        ((at_x, 0, ((y, pair),)), (at_a, 1, ((y, pair),)), (at_b, 2, ((y, pair),))),
        ((at_a, 0, ((y, every),)), (at_b, 1, ((ypair, pair),)), (at_x, 2, ((y, pair), (3 - y, pair)))),
        ((at_b, 0, ((ypair, every),)), (at_x, 1, ((every, pair),)), (at_a, 2, ((y, every), (3 - y, every)))),
    )
    held = tuple((p, s) for _, p, s in plan[2])
    last = ((0, ((yother, every),)), (1, ((every, other),)), (2, ((ya, every), (3 - ya, every))))

    class Gather:
        def __init__(self, part):
            self.part, self.live = part, {}

        def go(self, step):
            rs_ = [(to, self.part(ys, xs, p)) for to, p, sets in plan[step] for ys, xs in sets]
            self.live[step] = [send(r, r, to) for to, r in rs_]

        def wait(self, step):
            for c in self.live.pop(step, ()):
                c.wait_recv()

        def forward(self, what):
            rs_ = [self.part(ys, xs, p) for p, sets in what for ys, xs in sets]
            self.live["f"] = self.live.get("f", []) + [send(r, r, at_core) for r in rs_]

    def up_part(zs, rows=slice(None)):
        return lambda ys, xs, p: U.at[k, zs, ys, xs, p, rows]

    phases = (0, pl.ds(1, 2))

    def dn_part(g, zs):
        return lambda ys, xs, p: D.at[phases[g], k, zs, ys, xs, :, pl.ds(128 * p, 128)]

    def dn_last(b, zs):
        return lambda ys, xs, p: D.at[b, k, zs, ys, xs, :, pl.ds(128 * p, 128)]

    def most(st, dr):
        return 4 if st == dr else 3

    def t_slice(zo, st):
        if st == 0:
            return T.at[zo % 4, pl.ds(2 * (zo // 4), 2), pl.ds(0, TA)]
        return T.at[zo % 4, 2 * (zo // 4) + lo, pl.ds(TA, TB)]

    sent, lo_live, seen = {}, [], set()

    def need(*name):
        if name not in seen:
            seen.add(name)
            sent[name].wait_recv()

    def t_origin(dr, d):
        return ring_z(-d if dr == 0 else d)

    def t_send(st, d):
        for dr in (0, 1):
            if d <= most(st, dr):
                if d > 1:
                    need("t", st, dr, d - 1)
                r = t_slice(t_origin(dr, d - 1), st)
                sent["t", st, dr, d] = send(r, r, at_z[dr])

    def t_lo(d):
        for dr in (0, 1):
            if d <= most(1, dr):
                need("t", 1, dr, d)
                t_to_lo(t_origin(dr, d))

    def t_to_lo(zo):
        r = t_slice(zo, 1)
        lo_live.append(send(r, r, at_lo))

    def project(b):
        w = jnp.concatenate([D[b, h].reshape(1024, 384) for h in (0, 1)], axis=1)
        o = lax.dot_general(H[...], w, (((1,), (1,)), ((), ())), preferred_element_type=F32)
        for j in range(8):
            O[b, j // 2, j % 2] = o[:, 128 * j:128 * j + 128].reshape(4, 80, 128)

    ring_base = slots(48)
    last_send, last_recv = slots(36), slots(36)
    own_send, own_recv = slots(12), slots(15)
    l_base = slots(24)
    cut = (slice(0, RA), slice(RA, 80))

    def far_dir(b, st, dr):
        return (b + st) % 2 == dr

    def term(b, st, t):
        return O[b, t % 4, :, pl.ds(2 * (t // 4), 2)]

    def ring_copies(b, st, dr, d):
        m = (b * 2 + dr) * 4
        S, Q = SA, QA
        src, i = S.at[m + d - 1], ring_base + 24 * st + m
        if d > 1:
            return [copy(src, Q.at[m + d - 1], at_z[dr], i + d - 1)]
        zt = ring_z(1 if dr == 0 else -1)
        if True:
            return [copy(src.at[c, l], FA.at[b, dr, k, lo], dev(2 * hi + l, y, zt, c),
                         last_send + m + 2 * c + l, last_recv + m + 2 * k + lo)
                    for c in (0, 1) for l in (0, 1)]

    def ring(b, st, step):
        S, Q = SA, QA
        for dr in (0, 1):
            d = (4 if far_dir(b, st, dr) else 3) - step
            if d == 0:
                continue
            m = (b * 2 + dr) * 4
            v = term(b, st, ring_z(d if dr == 0 else -d))
            if step:
                ring_copies(b, st, dr, d + 1)[0].wait_recv()
                v = v + Q[m + d].astype(F32)
            S[m + d - 1] = v.astype(BF)
            for c in ring_copies(b, st, dr, d):
                c.start()
                pending.append(c.wait_send)

    def own(b):
        SO[b] = O[b, zl, :, pl.ds(2 * zh, 2), 0:RA].astype(BF)
        for i, (l, c) in enumerate(((lo, 1 - k), (1 - lo, k), (1 - lo, 1 - k))):
            send(SO.at[b, c, l], OA.at[b, k, lo], dev(2 * hi + l, y, z, c), own_send + 4 * b + i, own_recv + 5 * b + 2 * k + lo)

    def up32(r):
        return r.astype(F32)

    def finish(b):
        for l in (0, 1):
            landed(OA.at[b, 1 - k, l], own_recv + 5 * b + 2 * (1 - k) + l)
        landed(OA.at[b, k, 1 - lo], own_recv + 5 * b + 2 * k + 1 - lo)
        for kk in (1 - k, k):
            if kk is k:
                v = O[b, zl, k, 2 * zh + lo, 0:RA] + up32(OA[b, k, 1 - lo])
            else:
                v = up32(OA[b, kk, 0]) + up32(OA[b, kk, 1])
            for dr in (0, 1):
                for l in (0, 1):
                    landed(FA.at[b, dr, kk, l], last_recv + (b * 2 + dr) * 4 + 2 * kk + l)
                    v = v + up32(FA[b, dr, kk, l])
            V[kk, 0:RA, 128 * b:128 * b + 128] = v.astype(BF)

    def order():
        i = lax.broadcasted_iota(jnp.int32, (384, 384), 0)
        j = lax.broadcasted_iota(jnp.int32, (384, 384), 1)
        E[...] = (j == 96 * ((i % 128) // 32) + 32 * (i // 128) + i % 32).astype(F32).astype(BF)

    def pre(zs, first):
        for h in (0, 1):
            v = None if first else acc[h]
            for j in (0, 1):
                o = jnp.dot(T[2 * zs + j].reshape(320, 768), U[h, zs, 2 * j:2 * j + 2].reshape(768, 384),
                            preferred_element_type=F32)
                v = o if v is None else v + o
            acc[h] = v

    def act(j, carry):
        r = pl.ds(pl.multiple_of(j * 80, 16), 80)
        for h in (0, 1):
            v = acc[h, r, :]
            H[r, h * 384:(h + 1) * 384] = (v * (1.0 + lax.erf(v * 0.7071067811865476)) * 0.5).astype(BF)
        return carry

    rows_of = lambda c: pl.ds(pl.multiple_of(c * 80, 16), 80)
    lane = pl.ds(pl.multiple_of(k * 384, 128), 384)
    q_own = 2 * zh + lo
    t_dst = T.at[zl, q_own, :, lane]
    own_copy = pltpu.make_async_copy(tok.at[rows_of(k)], t_dst, rs.at[slots(1)])
    arrived = {}
    halves = (pl.ds(0, 16), pl.ds(16, 16))
    un = Gather(up_part(zh))
    uf = [Gather(up_part(1 - zh, r)) for r in halves]
    dn_g = [Gather(dn_part(g, zh)) for g in (0, 1)]
    df_g = [Gather(dn_part(g, 1 - zh)) for g in (0, 1)]
    dh_g = [Gather(dn_part(g, pl.ds(0, 2))) for g in (0, 1)]
    near = [Gather(dn_last(b, zh)) for b in range(3)]
    far = [Gather(dn_last(b, 1 - zh)) for b in range(3)]
    both = [Gather(dn_last(b, pl.ds(0, 2))) for b in range(3)]

    def ready(what, zs):
        if (what, zs is zh) not in seen:
            seen.add((what, zs is zh))
            arrived[what](zs)

    def tokens_in():
        sent["tc",] = send(tok.at[rows_of(1 - k)], t_dst, at_core)
        own_copy.start()

    def tokens_here():
        if "own" not in seen:
            seen.add("own")
            own_copy.wait()
        need("tc")

    def gather_step(G, what, zs, step):
        if step == 0:
            ready(what, zs)
        else:
            G.wait(step - 1)
        G.go(step)

    def tokens_all():
        if "all" not in seen:
            seen.add("all")
            for c in lo_live:
                c.wait_recv()
            for dr in (0, 1):
                need("t", 0, dr, most(0, dr))

    def hidden():
        for G in uf:
            G.wait("f")
        pre(1 - zh, False)
        lax.fori_loop(0, 4, act, 0)

    def run(op):
        kind, n = op[0], op[1:]
        if op[:2] == "uS":
            i = int(op[2])
            arrived["u", i] = spread(up.at[:, halves[i]], lambda h, zs, xs: U.at[h, zs, y, xs, :, halves[i]])
        elif op == "Tc":
            tokens_in()
        elif op == "T0lo":
            tokens_here()
            r = T.at[zl, q_own, pl.ds(0, TA)]
            sent["lo",] = send(r, r, at_lo)
        elif op == "Tl0":
            tokens_here()
            t_to_lo(z)
        elif op[:2] == "Tl":
            t_lo(int(op[2]))
        elif kind == "T":
            if op == "T01":
                need("lo")
            if op == "T11":
                tokens_here()
            t_send(int(op[1]), int(op[2]))
        elif op[:2] == "dS":
            g = int(op[2])
            arrived["d", g] = spread(dn.at[phases[g]], lambda h, zs, xs: D.at[phases[g], h, zs, y, xs])
        elif kind == "u":
            i = 0 if op[1] == "n" else int(op[2])
            G, zs, what = (un, zh, op[2:]) if op[1] == "n" else (uf[i], 1 - zh, op[3:])
            if what == "h":
                G.wait(1)
                G.forward(held)
            elif what == "l":
                G.wait(2)
                G.forward(last)
            else:
                if what == "1":
                    for j in ((0, 1) if op[1] == "n" else (i,)):
                        ready(("u", j), zs)
                else:
                    G.wait(int(what) - 2)
                G.go(int(what) - 1)
        elif op == "qre":
            tokens_all()
            un.wait("f")
            pre(zh, True)
        elif op[:2] == "dh":
            g = int(op[2])
            dn_g[g].wait(1)
            df_g[g].wait(1)
            dh_g[g].forward(held)
        elif op[:2] == "dl":
            b = int(op[2])
            near[b].wait(2)
            far[b].wait(2)
            both[b].forward(last)
        elif kind == "d":
            i = int(op[2])
            G, zs, L = (dn_g, zh, near) if op[1] == "n" else (df_g, 1 - zh, far)
            if op[3:] == "3x":
                G[min(i, 1)].wait(1)
                L[i].go(2)
            else:
                gather_step(G[i], ("d", i), zs, int(op[3]) - 1)
        elif op == "pre":
            hidden()
        elif kind == "p":
            b = int(n)
            dh_g[min(b, 1)].wait("f")
            both[b].wait("f")
            project(b)
        elif kind == "r":
            ring(int(n[0]), 0, int(n[1]))
        elif kind == "f":
            finish(int(n))

    starts = [op for op in ORDER if op[0] == "r" and op[2] == "0"]
    for op in ORDER:
        if op == "un1":
            order()
        run(op)
        if op == starts[-1]:
            for first in starts:
                own(int(first[1]))
    out[...] = jnp.dot(V[...].reshape(160, 384), E[...], preferred_element_type=F32).astype(BF)
    for w in pending:
        w()


def local(tokens, up_weight, down_weight):
    vmem = pl.BlockSpec(memory_space=pltpu.VMEM)
    hbm = pl.BlockSpec(memory_space=pltpu.HBM)
    out = pl.pallas_call(
        body,
        out_shape=jax.ShapeDtypeStruct((160, 384), BF),
        in_specs=[hbm] * 3,
        out_specs=vmem,
        scratch_shapes=[
            pltpu.VMEM((160, 384), BF),
            pltpu.VMEM((3, 32, 1536), BF),
            pltpu.VMEM((3, 32, 1536), BF),
            pltpu.VMEM((4, 4, 80, 768), BF),
            pltpu.VMEM((2, 2, 4, 4, 3, 32, 384), BF),
            pltpu.VMEM((3, 2, 2, 4, 4, 32, 384), BF),
            pltpu.VMEM((2, 320, 384), F32),
            pltpu.VMEM((320, 768), BF),
            pltpu.VMEM((3, 4, 2, 4, 80, 128), F32),
            pltpu.VMEM((24, 2, 2, RA, 128), BF),
            pltpu.VMEM((24, 2, 2, RA, 128), BF),
            pltpu.VMEM((3, 2, 2, 2, RA, 128), BF),
            pltpu.VMEM((3, 2, 2, RA, 128), BF),
            pltpu.VMEM((3, 2, 2, RA, 128), BF),
            pltpu.VMEM((2, 80, 384), BF),
            pltpu.VMEM((384, 384), BF),
            pltpu.SemaphoreType.DMA((SEMS,)),
            pltpu.SemaphoreType.DMA((SEMS,)),
            pltpu.SemaphoreType.DMA((3,)),
        ],
        compiler_params=pltpu.CompilerParams(
            collective_id=0, has_side_effects=True, vmem_limit_bytes=55040 << 10),
        name="ffn",
    )(tokens, up_weight.reshape(3, 32, 1536), down_weight.T.reshape(3, 32, 1536))
    return out


def solution(mesh):
    return jax.shard_map(
        local,
        mesh=mesh,
        in_specs=(P("row", "col"), P("row", "col"), P("col", "row")),
        out_specs=P("row", "col"),
        check_vma=False,
    )
```

```python
import jax
import jax.numpy as jnp
from jax import lax
from jax.experimental import pallas as pl
from jax.experimental.pallas import tpu as pltpu
from jax.sharding import PartitionSpec as P

MESH = pl.DeviceIdType.MESH
BF = jnp.bfloat16
F32 = jnp.float32
TA, TB = 32, 48
RA, RB = 80, 0
SEMS = 460
ORDER = (
    "uS1", "Tc", "uS0", "T11", "dS1", "un1", "dn11", "T0lo",
    "uf11", "un2", "uf01", "uf12", "dn12", "T01", "un3", "T12",
    "dS0", "df11", "Tl1", "uf1h", "Tl0", "dn01", "T02", "uf02",
    "unh", "uf13", "Tl2", "T13", "df01", "df12", "dn02", "T03",
    "T14", "uf03", "Tl3", "df02", "dn23x", "unl", "T04", "df23x",
    "uf1l", "dn03x", "Tl4", "uf0l", "df03x", "df13x", "uf0h", "dh0",
    "dn13x", "dl2", "dh1", "qre", "pre", "dl0", "p2", "r20",
    "dl1", "p0", "r00", "p1", "r10", "r21", "r01", "r11",
    "r22", "r02", "r12", "r23", "r03", "r13", "f2", "f0",
    "f1",
)


def dev(x, y, z, k):
    return ((z // 4) * 16 + y * 4 + x, (z % 4) * 2 + k)


def body(tok_h, up_h, dn_h, out, tok, up, dn, T, U, D, acc, H, O, SA, QA, FA, SO, OA, V, E, ss, rs, ls):
    row = lax.axis_index("row")
    col = lax.axis_index("col")
    x, y, zh = row % 4, (row // 4) % 4, row // 16
    zl, k = col // 2, col % 2
    z = 4 * zh + zl
    hi, lo = x // 2, x % 2
    yh, yl = y // 2, y % 2
    ya = 2 * yh + 1 - yl
    turn = ((x + 1) // 2) % 2
    x_lo = 2 * hi + 1 - lo

    def ring_z(n):
        return (z + 8 + n) % 8

    at_core = dev(x, y, z, 1 - k)
    at_lo = dev(x_lo, y, z, k)
    at_x = dev(3 - x, y, z, k)
    at_a = dev(x, ya, z, k)
    at_b = dev(x, 3 - y, z, k)
    at_z = (dev(x, y, ring_z(1), k), dev(x, y, ring_z(-1), k))

    loads = [pltpu.make_async_copy(a, b, ls.at[i]) for i, (a, b) in enumerate(((up_h, up), (tok_h, tok), (dn_h, dn)))]
    for c in loads:
        c.start()
    barrier = pltpu.get_barrier_semaphore()
    friends = [at_x, at_a, at_b]
    for n in (0, 4, 1, -1):
        for px in (x, x_lo):
            for pk in (k, 1 - k):
                if n or px is not x or pk is not k:
                    friends.append(dev(px, y, ring_z(n), pk))
    for f in friends:
        pl.semaphore_signal(barrier, inc=1, device_id=f, device_id_type=MESH)
    pl.semaphore_wait(barrier, len(friends))
    for c in loads:
        c.wait()

    count = [0]
    pending = []

    def slots(n):
        first = count[0]
        count[0] += n
        assert count[0] <= SEMS
        return first

    def copy(src, dst, to, i, j=None):
        return pltpu.make_async_remote_copy(
            src_ref=src, dst_ref=dst, send_sem=ss.at[i], recv_sem=rs.at[i if j is None else j],
            device_id=to, device_id_type=MESH)

    def send(src, dst, to, i=None, j=None):
        c = copy(src, dst, to, slots(1) if i is None else i, j)
        c.start()
        pending.append(c.wait_send)
        return c

    def landed(ref, i):
        pltpu.make_async_copy(ref, ref, rs.at[i]).wait()

    def spread(S, at):
        base = slots(4)
        far = zh + k - 2 * zh * k
        for g in (0, 1):
            for h in (0, 1):
                src = S.at[..., pl.ds((2 * g + h) * 384, 384)]
                dst = at(h, zh, x)
                to = dev(2 * hi + (1 - hi if g else hi), y, 4 * k + zl, h)
                own = (far == 0) & (turn == g) & (k == h)

                def c(src=src, dst=dst, to=to, i=base + 2 * g + h):
                    return copy(src, dst, to, i, base + 2 * far + lo)

                @pl.when(own)
                def _():
                    pltpu.make_async_copy(src, dst, rs.at[base + 2 * far + lo]).start()

                @pl.when(jnp.logical_not(own))
                def _():
                    c().start()

                def done(own=own, c=c):
                    @pl.when(jnp.logical_not(own))
                    def _():
                        c().wait_send()
                pending.append(done)

        def arrived(zs):
            off = zs + zh - 2 * zs * zh
            for l in (0, 1):
                landed(at(k, zs, 2 * hi + l), base + 2 * off + l)
        return arrived

    pair, other = pl.ds(2 * hi, 2), pl.ds(2 - 2 * hi, 2)
    ypair, yother = pl.ds(2 * yh, 2), pl.ds(2 - 2 * yh, 2)
    every = pl.ds(0, 4)
    plan = (
        ((at_x, 0, ((y, pair),)), (at_a, 1, ((y, pair),)), (at_b, 2, ((y, pair),))),
        ((at_a, 0, ((y, every),)), (at_b, 1, ((ypair, pair),)), (at_x, 2, ((y, pair), (3 - y, pair)))),
        ((at_b, 0, ((ypair, every),)), (at_x, 1, ((every, pair),)), (at_a, 2, ((y, every), (3 - y, every)))),
    )
    held = tuple((p, s) for _, p, s in plan[2])
    last = ((0, ((yother, every),)), (1, ((every, other),)), (2, ((ya, every), (3 - ya, every))))

    class Gather:
        def __init__(self, part):
            self.part, self.live = part, {}

        def go(self, step):
            rs_ = [(to, self.part(ys, xs, p)) for to, p, sets in plan[step] for ys, xs in sets]
            self.live[step] = [send(r, r, to) for to, r in rs_]

        def wait(self, step):
            for c in self.live.pop(step, ()):
                c.wait_recv()

        def forward(self, what):
            rs_ = [self.part(ys, xs, p) for p, sets in what for ys, xs in sets]
            self.live["f"] = self.live.get("f", []) + [send(r, r, at_core) for r in rs_]

    def up_part(zs, rows=slice(None)):
        return lambda ys, xs, p: U.at[k, zs, ys, xs, p, rows]

    phases = (0, pl.ds(1, 2))

    def dn_part(g, zs):
        return lambda ys, xs, p: D.at[phases[g], k, zs, ys, xs, :, pl.ds(128 * p, 128)]

    def dn_last(b, zs):
        return lambda ys, xs, p: D.at[b, k, zs, ys, xs, :, pl.ds(128 * p, 128)]

    def most(st, dr):
        return 4 if st == dr else 3

    def t_slice(zo, st):
        if st == 0:
            return T.at[zo % 4, pl.ds(2 * (zo // 4), 2), pl.ds(0, TA)]
        return T.at[zo % 4, 2 * (zo // 4) + lo, pl.ds(TA, TB)]

    sent, lo_live, seen = {}, [], set()

    def need(*name):
        if name not in seen:
            seen.add(name)
            sent[name].wait_recv()

    def t_origin(dr, d):
        return ring_z(-d if dr == 0 else d)

    def t_send(st, d):
        for dr in (0, 1):
            if d <= most(st, dr):
                if d > 1:
                    need("t", st, dr, d - 1)
                r = t_slice(t_origin(dr, d - 1), st)
                sent["t", st, dr, d] = send(r, r, at_z[dr])

    def t_lo(d):
        for dr in (0, 1):
            if d <= most(1, dr):
                need("t", 1, dr, d)
                t_to_lo(t_origin(dr, d))

    def t_to_lo(zo):
        r = t_slice(zo, 1)
        lo_live.append(send(r, r, at_lo))

    def project(b):
        w = jnp.concatenate([D[b, h].reshape(1024, 384) for h in (0, 1)], axis=1)
        o = lax.dot_general(H[...], w, (((1,), (1,)), ((), ())), preferred_element_type=F32)
        for j in range(8):
            O[b, j // 2, j % 2] = o[:, 128 * j:128 * j + 128].reshape(4, 80, 128)

    ring_base = slots(48)
    last_send, last_recv = slots(36), slots(36)
    own_send, own_recv = slots(12), slots(15)
    l_base = slots(24)
    cut = (slice(0, RA), slice(RA, 80))

    def far_dir(b, st, dr):
        return (b + st) % 2 == dr

    def term(b, st, t):
        return O[b, t % 4, :, pl.ds(2 * (t // 4), 2)]

    def ring_copies(b, st, dr, d):
        m = (b * 2 + dr) * 4
        S, Q = SA, QA
        src, i = S.at[m + d - 1], ring_base + 24 * st + m
        if d > 1:
            return [copy(src, Q.at[m + d - 1], at_z[dr], i + d - 1)]
        zt = ring_z(1 if dr == 0 else -1)
        if True:
            return [copy(src.at[c, l], FA.at[b, dr, k, lo], dev(2 * hi + l, y, zt, c),
                         last_send + m + 2 * c + l, last_recv + m + 2 * k + lo)
                    for c in (0, 1) for l in (0, 1)]

    def ring(b, st, step):
        S, Q = SA, QA
        for dr in (0, 1):
            d = (4 if far_dir(b, st, dr) else 3) - step
            if d == 0:
                continue
            m = (b * 2 + dr) * 4
            v = term(b, st, ring_z(d if dr == 0 else -d))
            if step:
                ring_copies(b, st, dr, d + 1)[0].wait_recv()
                v = v + Q[m + d].astype(F32)
            S[m + d - 1] = v.astype(BF)
            for c in ring_copies(b, st, dr, d):
                c.start()
                pending.append(c.wait_send)

    def own(b):
        SO[b] = O[b, zl, :, pl.ds(2 * zh, 2), 0:RA].astype(BF)
        for i, (l, c) in enumerate(((lo, 1 - k), (1 - lo, k), (1 - lo, 1 - k))):
            send(SO.at[b, c, l], OA.at[b, k, lo], dev(2 * hi + l, y, z, c), own_send + 4 * b + i, own_recv + 5 * b + 2 * k + lo)

    def up32(r):
        return r.astype(F32)

    def finish(b):
        for l in (0, 1):
            landed(OA.at[b, 1 - k, l], own_recv + 5 * b + 2 * (1 - k) + l)
        landed(OA.at[b, k, 1 - lo], own_recv + 5 * b + 2 * k + 1 - lo)
        for kk in (1 - k, k):
            if kk is k:
                v = O[b, zl, k, 2 * zh + lo, 0:RA] + up32(OA[b, k, 1 - lo])
            else:
                v = up32(OA[b, kk, 0]) + up32(OA[b, kk, 1])
            for dr in (0, 1):
                for l in (0, 1):
                    landed(FA.at[b, dr, kk, l], last_recv + (b * 2 + dr) * 4 + 2 * kk + l)
                    v = v + up32(FA[b, dr, kk, l])
            V[kk, 0:RA, 128 * b:128 * b + 128] = v.astype(BF)

    def order():
        i = lax.broadcasted_iota(jnp.int32, (384, 384), 0)
        j = lax.broadcasted_iota(jnp.int32, (384, 384), 1)
        E[...] = (j == 96 * ((i % 128) // 32) + 32 * (i // 128) + i % 32).astype(F32).astype(BF)

    def pre(zs, h, first):
        v = None if first else acc[h]
        for j in (0, 1):
            o = jnp.dot(T[2 * zs + j].reshape(320, 768), U[h, zs, 2 * j:2 * j + 2].reshape(768, 384),
                        preferred_element_type=F32)
            v = o if v is None else v + o
        acc[h] = v

    def act(h):
        lanes = pl.ds(pl.multiple_of(h * 384, 128), 384)

        def step(j, carry):
            r = pl.ds(pl.multiple_of(j * 80, 16), 80)
            v = acc[h, r, :]
            H[r, lanes] = (v * (1.0 + lax.erf(v * 0.7071067811865476)) * 0.5).astype(BF)
            return carry
        lax.fori_loop(0, 4, step, 0)

    rows_of = lambda c: pl.ds(pl.multiple_of(c * 80, 16), 80)
    lane = pl.ds(pl.multiple_of(k * 384, 128), 384)
    q_own = 2 * zh + lo
    t_dst = T.at[zl, q_own, :, lane]
    own_copy = pltpu.make_async_copy(tok.at[rows_of(k)], t_dst, rs.at[slots(1)])
    arrived = {}
    halves = (pl.ds(0, 16), pl.ds(16, 16))
    un = Gather(up_part(zh))
    uf = [Gather(up_part(1 - zh, r)) for r in halves]
    dn_g = [Gather(dn_part(g, zh)) for g in (0, 1)]
    df_g = [Gather(dn_part(g, 1 - zh)) for g in (0, 1)]
    dh_g = [Gather(dn_part(g, pl.ds(0, 2))) for g in (0, 1)]
    near = [Gather(dn_last(b, zh)) for b in range(3)]
    far = [Gather(dn_last(b, 1 - zh)) for b in range(3)]
    both = [Gather(dn_last(b, pl.ds(0, 2))) for b in range(3)]

    def ready(what, zs):
        if (what, zs is zh) not in seen:
            seen.add((what, zs is zh))
            arrived[what](zs)

    def tokens_in():
        sent["tc",] = send(tok.at[rows_of(1 - k)], t_dst, at_core)
        own_copy.start()

    def tokens_here():
        if "own" not in seen:
            seen.add("own")
            own_copy.wait()
        need("tc")

    def gather_step(G, what, zs, step):
        if step == 0:
            ready(what, zs)
        else:
            G.wait(step - 1)
        G.go(step)

    def tokens_all():
        if "all" not in seen:
            seen.add("all")
            for c in lo_live:
                c.wait_recv()
            for dr in (0, 1):
                need("t", 0, dr, most(0, dr))

    def hidden():
        pre(1 - zh, k, False)
        act(k)
        for G in uf:
            G.wait("f")
        pre(1 - zh, 1 - k, False)
        act(1 - k)

    def run(op):
        kind, n = op[0], op[1:]
        if op[:2] == "uS":
            i = int(op[2])
            arrived["u", i] = spread(up.at[:, halves[i]], lambda h, zs, xs: U.at[h, zs, y, xs, :, halves[i]])
        elif op == "Tc":
            tokens_in()
        elif op == "T0lo":
            tokens_here()
            r = T.at[zl, q_own, pl.ds(0, TA)]
            sent["lo",] = send(r, r, at_lo)
        elif op == "Tl0":
            tokens_here()
            t_to_lo(z)
        elif op[:2] == "Tl":
            t_lo(int(op[2]))
        elif kind == "T":
            if op == "T01":
                need("lo")
            if op == "T11":
                tokens_here()
            t_send(int(op[1]), int(op[2]))
        elif op[:2] == "dS":
            g = int(op[2])
            arrived["d", g] = spread(dn.at[phases[g]], lambda h, zs, xs: D.at[phases[g], h, zs, y, xs])
        elif kind == "u":
            i = 0 if op[1] == "n" else int(op[2])
            G, zs, what = (un, zh, op[2:]) if op[1] == "n" else (uf[i], 1 - zh, op[3:])
            if what == "h":
                G.wait(1)
                G.forward(held)
            elif what == "l":
                G.wait(2)
                G.forward(last)
            else:
                if what == "1":
                    for j in ((0, 1) if op[1] == "n" else (i,)):
                        ready(("u", j), zs)
                else:
                    G.wait(int(what) - 2)
                G.go(int(what) - 1)
        elif op == "qre":
            tokens_all()
            un.wait("f")
            for h in (0, 1):
                pre(zh, h, True)
        elif op[:2] == "dh":
            g = int(op[2])
            dn_g[g].wait(1)
            df_g[g].wait(1)
            dh_g[g].forward(held)
        elif op[:2] == "dl":
            b = int(op[2])
            near[b].wait(2)
            far[b].wait(2)
            both[b].forward(last)
        elif kind == "d":
            i = int(op[2])
            G, zs, L = (dn_g, zh, near) if op[1] == "n" else (df_g, 1 - zh, far)
            if op[3:] == "3x":
                G[min(i, 1)].wait(1)
                L[i].go(2)
            else:
                gather_step(G[i], ("d", i), zs, int(op[3]) - 1)
        elif op == "pre":
            hidden()
        elif kind == "p":
            b = int(n)
            dh_g[min(b, 1)].wait("f")
            both[b].wait("f")
            project(b)
        elif kind == "r":
            ring(int(n[0]), 0, int(n[1]))
        elif kind == "f":
            finish(int(n))

    starts = [op for op in ORDER if op[0] == "r" and op[2] == "0"]
    for op in ORDER:
        if op == "un1":
            order()
        run(op)
        if op == starts[-1]:
            for first in starts:
                own(int(first[1]))
    out[...] = jnp.dot(V[...].reshape(160, 384), E[...], preferred_element_type=F32).astype(BF)
    for w in pending:
        w()


def local(tokens, up_weight, down_weight):
    vmem = pl.BlockSpec(memory_space=pltpu.VMEM)
    hbm = pl.BlockSpec(memory_space=pltpu.HBM)
    out = pl.pallas_call(
        body,
        out_shape=jax.ShapeDtypeStruct((160, 384), BF),
        in_specs=[hbm] * 3,
        out_specs=vmem,
        scratch_shapes=[
            pltpu.VMEM((160, 384), BF),
            pltpu.VMEM((3, 32, 1536), BF),
            pltpu.VMEM((3, 32, 1536), BF),
            pltpu.VMEM((4, 4, 80, 768), BF),
            pltpu.VMEM((2, 2, 4, 4, 3, 32, 384), BF),
            pltpu.VMEM((3, 2, 2, 4, 4, 32, 384), BF),
            pltpu.VMEM((2, 320, 384), F32),
            pltpu.VMEM((320, 768), BF),
            pltpu.VMEM((3, 4, 2, 4, 80, 128), F32),
            pltpu.VMEM((24, 2, 2, RA, 128), BF),
            pltpu.VMEM((24, 2, 2, RA, 128), BF),
            pltpu.VMEM((3, 2, 2, 2, RA, 128), BF),
            pltpu.VMEM((3, 2, 2, RA, 128), BF),
            pltpu.VMEM((3, 2, 2, RA, 128), BF),
            pltpu.VMEM((2, 80, 384), BF),
            pltpu.VMEM((384, 384), BF),
            pltpu.SemaphoreType.DMA((SEMS,)),
            pltpu.SemaphoreType.DMA((SEMS,)),
            pltpu.SemaphoreType.DMA((3,)),
        ],
        compiler_params=pltpu.CompilerParams(
            collective_id=0, has_side_effects=True, vmem_limit_bytes=55040 << 10),
        name="ffn",
    )(tokens, up_weight.reshape(3, 32, 1536), down_weight.T.reshape(3, 32, 1536))
    return out


def solution(mesh):
    return jax.shard_map(
        local,
        mesh=mesh,
        in_specs=(P("row", "col"), P("row", "col"), P("col", "row")),
        out_specs=P("row", "col"),
        check_vma=False,
    )
```
